32 devices in a mesh: groups: 2 (over y), shard: 4 (over z), mirror: 4 (over x, core).
Axes of the slice: x: 2, y: 2, z: 4, core: 2. Of those that a mesh axis runs over, the one named last changes fastest.
Arguments:
- embeddings: bfloat16 [16384, 1024], P(('groups', 'shard', 'mirror')), parts along dimension 0, may hold values from -6 to 6
- assignment: int32 [16384], P(('groups', 'shard', 'mirror')), parts along dimension 0, may hold values from 0 to 15, as said below
- counts: int32 [32], P('groups'), parts along dimension 0, may hold values from 64 to 1024, as said below
- slot: int32 [16384], P(('groups', 'shard', 'mirror')), parts along dimension 0, may hold values from 0 to 63, as said below
Outputs:
- dup_score: float32 [16384], P(('groups', 'shard', 'mirror')), parts along dimension 0
- centroids: float32 [32, 1024], P('groups'), parts along dimension 0
The draws below stay inside these ranges and needn't reach their ends.
There are 2 independent parts, one for each index of `groups`. The reference program is written for one: setup_inputs(seed, part) draws one part's arguments, and reference() takes and returns one part's arrays. A program takes and returns all parts, laid end to end along the dimension named above; each array names one. Nothing has to cross between parts.
Inputs may be any that keep to these rules, and one draw needn't show every extreme that they name: `assignment`: among the rows of one device (aligned blocks of 512 rows), at most 64 name one cluster; one cluster is named by exactly 64 rows in every block, and every cluster has exactly 64 rows in some block. `slot`: the rows of one device that name the same cluster have distinct slots. counts[c] is the number of rows of the slab whose assignment is c.
All inputs are finite; a program needn't handle non-finite values.
Results may differ from the reference program's by a relative error of at most 0.0032.
Values may be sent and summed in bfloat16 or wider, within the bound.
A program may use at most 64 MiB of HBM per device.

```python
import jax
import jax.numpy as jnp
from jax import lax

D = 1024
ROWS_DEV = 512
BLOCKS = 16
CLUSTERS = 16
CAP = 64
ROWS = 8192


def layout(key):
    offset = jax.random.randint(jax.random.fold_in(key, 11), (), 0, CLUSTERS)
    common = jax.random.randint(jax.random.fold_in(key, 13), (), 0, CLUSTERS)
    block_keys = jax.random.split(jax.random.fold_in(key, 12), BLOCKS)
    slot_ids = jnp.arange(CLUSTERS * CAP, dtype=jnp.int32)

    def one_block(block_key, block):
        first_key, second_key = jax.random.split(block_key)
        ranks = jax.random.permutation(first_key, CLUSTERS * CAP).astype(jnp.int32)
        filled = (block + offset) % CLUSTERS
        owner_of = slot_ids // CAP
        forced = (owner_of == filled) | (owner_of == common)
        score = ranks - jnp.where(forced, CLUSTERS * CAP, 0)
        chosen = jnp.argsort(score, stable=True)[:ROWS_DEV].astype(jnp.int32)
        chosen = chosen[jax.random.permutation(second_key, ROWS_DEV)]
        return (chosen // CAP, chosen % CAP)
    cluster_ids, slot_values = jax.vmap(one_block)(block_keys, jnp.arange(BLOCKS, dtype=jnp.int32))
    return (cluster_ids.reshape(ROWS).astype(jnp.int32), slot_values.reshape(ROWS).astype(jnp.int32))


def draw_assignment(key, part):
    cluster_ids, slot_values = layout(key)
    return cluster_ids


def draw_slot(key, part):
    cluster_ids, slot_values = layout(key)
    return slot_values


def draw_counts(key, part):
    cluster_ids, slot_values = layout(key)
    return jax.ops.segment_sum(jnp.ones((ROWS,), jnp.int32), cluster_ids, CLUSTERS).astype(jnp.int32)


def shard_levels(rng, extent, pieces, smallest, largest):
    def one(dim, shards_of):
        draws = jax.random.uniform(jax.random.fold_in(jax.random.fold_in(rng, 6), dim), (shards_of,), jnp.float32, smallest / len(pieces), largest / len(pieces))
        return jnp.repeat(jnp.exp(draws), extent[dim] // shards_of).reshape((-1,) + (1,) * (len(extent) - dim - 1))

    loudness = one(*pieces[0])
    for cut in pieces[1:]:
        loudness = loudness * one(*cut)
    return loudness


def noise(own_key, dims, spread, limit, cuts=(), held_as=jnp.bfloat16):
    values = jax.random.normal(own_key, dims, jnp.float32) * spread
    if len(cuts) > 0:
        values = shard_levels(own_key, dims, cuts, -0.22, 0.18) * values
    return jnp.clip(values, min=-limit, max=limit).astype(held_as)


def setup_inputs(seed: int = 0, part: int = 0) -> dict:
    key_list = jax.random.split(jax.random.key(seed), 5)
    part_splits = jax.random.split(jax.random.fold_in(key_list[4], part), 5)
    return {
        "embeddings": noise(part_splits[0], (ROWS, D), 1.0, 6.0, ((0, 16),)),
        "assignment": draw_assignment(jax.random.fold_in(jax.random.fold_in(key_list[4], part), 71), part),
        "counts": draw_counts(jax.random.fold_in(jax.random.fold_in(key_list[4], part), 71), part),
        "slot": draw_slot(jax.random.fold_in(jax.random.fold_in(key_list[4], part), 71), part),
    }


sharpness = 50.0

def reference(embeddings, assignment, counts, slot):
    wide = embeddings.astype(jnp.float32)
    unit_rows = (wide / jnp.sqrt(lax.optimization_barrier(jnp.sum(wide * wide, axis=1, keepdims=True)) + 1e-06)).astype(jnp.bfloat16)
    width = BLOCKS * CAP
    block_of = jnp.arange(ROWS, dtype=jnp.int32) // ROWS_DEV
    position = (block_of * CAP + slot).astype(jnp.int32)
    flat_index = (assignment * width + position).astype(jnp.int32)
    padded = jnp.zeros((CLUSTERS * width, D), jnp.bfloat16).at[flat_index].set(unit_rows)
    present = jnp.zeros((CLUSTERS * width,), jnp.float32).at[flat_index].set(1.0)
    diagonal = jnp.arange(width, dtype=jnp.int32)[:, None] == jnp.arange(width, dtype=jnp.int32)[None, :]

    def one_cluster(cluster):
        start = (cluster * width).astype(jnp.int32)
        members = lax.dynamic_slice_in_dim(padded, start, width, 0)
        valid = lax.dynamic_slice_in_dim(present, start, width, 0)
        cosine = jnp.dot(members, members.T, preferred_element_type=jnp.float32)
        weights = jnp.where(diagonal, 0.0, jnp.exp(sharpness * cosine) * valid[None, :])
        total = lax.optimization_barrier(jnp.sum(weights, axis=1))
        count_here = counts[cluster].astype(jnp.float32)
        return jnp.log(1.0 + total / count_here)
    scores = lax.map(one_cluster, jnp.arange(CLUSTERS, dtype=jnp.int32))
    dup_score = scores.reshape(-1)[flat_index]
    sums = jax.ops.segment_sum(unit_rows.astype(jnp.float32), assignment, CLUSTERS)
    centroids = sums / jnp.sqrt(lax.optimization_barrier(jnp.mean(sums * sums, axis=1, keepdims=True)) + 1e-06)
    return (dup_score, centroids)
```

```python
import functools

import jax
import jax.numpy as jnp
from jax import lax
from jax.experimental import pallas as pl
from jax.experimental.pallas import tpu as pltpu
from jax.sharding import PartitionSpec as P

sharpness = 50.0
f32, bf16 = jnp.float32, jnp.bfloat16


def flipped(index, mask):
    result, place = index, 1
    while place <= mask:
        if mask & place:
            bit = lax.rem(lax.div(index, place), 2)
            result = result + place * (1 - 2 * bit)
        place *= 2
    return result


def visiting_order(shards, mirrors):
    masks = [dz * mirrors + dm for dz in range(shards) for dm in range(mirrors)]
    far = lambda mask: (-(mask // mirrors), mask % mirrors)
    return [0] + sorted([m for m in masks if m], key=far)


def kernel(
    shards,
    mirrors,
    emb_ref,
    assign_ref,
    slot_ref,
    counts_ref,
    score_ref,
    cent_ref,
    place,
    outgoing,
    members,
    total,
    score_out,
    score_in,
    cent_all,
    row_send,
    row_recv,
    score_send,
    score_recv,
    cent_send,
    cent_recv,
):
    n = shards * mirrors
    rows, features = emb_ref.shape
    width = members.shape[0]
    cap = width // n
    pair = 2 * cap
    order = visiting_order(shards, mirrors)
    my_shard, my_mirror = lax.axis_index("shard"), lax.axis_index("mirror")
    me = my_shard * mirrors + my_mirror

    def peer(q):
        return {
            "shard": flipped(my_shard, order[q] // mirrors),
            "mirror": flipped(my_mirror, order[q] % mirrors),
        }

    def remote(src, dst, send, recv, q):
        return pltpu.make_async_remote_copy(
            src_ref=src,
            dst_ref=dst,
            send_sem=send.at[q],
            recv_sem=recv.at[q],
            device_id=peer(q),
            device_id_type=pl.DeviceIdType.MESH,
        )

    barrier = pltpu.get_barrier_semaphore()
    for q in range(1, n):
        pl.semaphore_signal(
            barrier, inc=1, device_id=peer(q), device_id_type=pl.DeviceIdType.MESH
        )

    wide = emb_ref[...].astype(f32)
    square = jnp.sum(wide * wide, axis=1, keepdims=True) + 1e-06
    unit_rows = (wide * (1.0 / jnp.sqrt(square))).astype(bf16)
    mask_of = assign_ref[...] ^ me
    position = jnp.zeros_like(mask_of)
    for q in range(n):
        position = jnp.where(mask_of == order[q], q, position)
    flat_slot = position * cap + slot_ref[...]

    row_copies = {
        q: remote(
            outgoing.at[pl.ds(q * cap, cap)],
            members.at[pl.ds(q * cap, cap)],
            row_send,
            row_recv,
            q,
        )
        for q in range(1, n)
    }
    batch = 4
    for first in range(0, n, batch):
        span = batch * cap
        slots = lax.broadcasted_iota(jnp.int32, (span, rows), 0) + first * cap
        hot = jnp.where(slots == flat_slot, 1.0, 0.0).astype(bf16)
        place[pl.ds(first * cap, span), :] = hot
        block = jnp.dot(hot, unit_rows, preferred_element_type=f32).astype(bf16)
        if first == 0:
            members[pl.ds(0, cap), :] = block[:cap]
            outgoing[pl.ds(cap, span - cap), :] = block[cap:]
            pl.semaphore_wait(barrier, n - 1)
        else:
            outgoing[pl.ds(first * cap, span), :] = block
        for q in range(max(first, 1), first + batch):
            row_copies[q].start()

    count = jnp.sum(
        jnp.where(
            lax.broadcasted_iota(jnp.int32, counts_ref.shape, 1) == me, counts_ref[...], 0
        ),
        axis=1,
        keepdims=True,
    ).astype(f32)

    def cosine(a, b):
        return lax.dot_general(a, b, (((1,), (1,)), ((), ())), preferred_element_type=f32)

    def fold(x):
        return jnp.sum(x.reshape(x.shape[0] // 8, 8, x.shape[1]), axis=0)

    own = lax.broadcasted_iota(jnp.int32, (pair, pair), 0) == lax.broadcasted_iota(
        jnp.int32, (pair, pair), 1
    )
    sums = jnp.zeros((8, features), f32)
    for p in range(n // 2):
        for q in (2 * p, 2 * p + 1):
            if q > 0:
                row_copies[q].wait_recv()
        fresh = members[pl.ds(p * pair, pair), :]
        sums = sums + fold(fresh.astype(f32))
        within = jnp.where(own, 0.0, jnp.exp(sharpness * cosine(fresh, fresh)) - 1.0)
        gained = fold(within)
        if p > 0:
            old = members[pl.ds(0, p * pair), :]
            gained = gained + fold(jnp.exp(sharpness * cosine(old, fresh)) - 1.0)
            total[:, pl.ds(0, p * pair)] += fold(jnp.exp(sharpness * cosine(fresh, old)) - 1.0)
        total[:, pl.ds(p * pair, pair)] = gained

    sum_row = jnp.sum(sums, axis=0, keepdims=True)
    cent_all[me] = sum_row / jnp.sqrt(jnp.mean(sum_row * sum_row, axis=1, keepdims=True) + 1e-06)
    cent_copies = {
        q: remote(cent_all.at[me], cent_all.at[me], cent_send, cent_recv, q) for q in range(1, n)
    }
    for q in range(1, n):
        cent_copies[q].start()

    sum_here = jnp.sum(total[...], axis=0, keepdims=True) + (count - 1.0)
    scores = jnp.log(1.0 + sum_here / count)
    for p in range(n // 2):
        score_out[p] = scores[:, p * pair : (p + 1) * pair]
    score_copies = {
        q: remote(score_out.at[q // 2], score_in.at[q], score_send, score_recv, q)
        for q in range(1, n)
    }
    for q in range(1, n):
        score_copies[q].start()

    score_in[0] = score_out[0]
    for q in range(1, n):
        score_copies[q].wait_recv()
    low = lax.broadcasted_iota(jnp.int32, (1, pair), 1) < cap
    returned = jnp.concatenate(
        [jnp.where(low, score_in[2 * p], score_in[2 * p + 1]) for p in range(n // 2)], axis=1
    )
    high = returned.astype(bf16)
    rest = returned - high.astype(f32)
    middle = rest.astype(bf16)
    little = (rest - middle.astype(f32)).astype(bf16)
    terms = jnp.concatenate(
        [high, middle, little, jnp.zeros((13, width), bf16)], axis=0
    )
    picked = jnp.dot(terms, place[...], preferred_element_type=f32)
    score_ref[...] = picked[0:1] + (picked[1:2] + picked[2:3])

    for q in range(1, n):
        cent_copies[q].wait_recv()
    for c in range(n):
        cent_ref[pl.ds(c, 1), :] = cent_all[c]
    for q in range(1, n):
        row_copies[q].wait_send()
        score_copies[q].wait_send()
        cent_copies[q].wait_send()


def fused(embeddings, assignment, counts, slot, capacity):
    shards, mirrors = lax.axis_size("shard"), lax.axis_size("mirror")
    n = shards * mirrors
    rows, features = embeddings.shape
    width = n * capacity
    vmem = pl.BlockSpec(memory_space=pltpu.VMEM)
    sems = [pltpu.SemaphoreType.DMA((n,))] * 6
    scores, centroids = pl.pallas_call(
        functools.partial(kernel, shards, mirrors),
        out_shape=(
            jax.ShapeDtypeStruct((1, rows), f32),
            jax.ShapeDtypeStruct((n, features), f32),
        ),
        in_specs=[vmem] * 4,
        out_specs=(vmem, vmem),
        scratch_shapes=[
            pltpu.VMEM((width, rows), bf16),
            pltpu.VMEM((width, features), bf16),
            pltpu.VMEM((width, features), bf16),
            pltpu.VMEM((8, width), f32),
            pltpu.VMEM((n // 2, 1, 2 * capacity), f32),
            pltpu.VMEM((n, 1, 2 * capacity), f32),
            pltpu.VMEM((n, 1, features), f32),
        ]
        + sems,
        compiler_params=pltpu.CompilerParams(
            collective_id=0, has_side_effects=True, vmem_limit_bytes=40 * 2**20
        ),
    )(embeddings, assignment[None, :], slot[None, :], counts[None, :])
    return scores.reshape(rows), centroids


def general(embeddings, assignment, counts, slot, capacity):
    shard_count = lax.axis_size("shard")
    mirror_count = lax.axis_size("mirror")
    rows_here, features = embeddings.shape
    clusters = counts.shape[0]
    width = shard_count * mirror_count * capacity

    def exchange(x):
        x = lax.all_to_all(x, "shard", split_axis=0, concat_axis=0, tiled=True)
        return lax.all_to_all(x, "mirror", split_axis=1, concat_axis=1, tiled=True)

    wide = embeddings.astype(f32)
    unit_rows = (wide / jnp.sqrt(jnp.sum(wide * wide, axis=1, keepdims=True) + 1e-06)).astype(bf16)
    cluster_ids = jnp.arange(clusters, dtype=jnp.int32)
    flat_slot = assignment * capacity + slot
    outgoing = jnp.zeros((width, features), bf16).at[flat_slot].set(unit_rows)
    present = jnp.zeros((width,), bf16).at[flat_slot].set(jnp.ones((rows_here,), bf16))
    members = exchange(outgoing.reshape(shard_count, mirror_count, capacity, features)).reshape(
        width, features
    )
    valid = exchange(present.reshape(shard_count, mirror_count, capacity)).reshape(width)
    owner = lax.axis_index("shard") * mirror_count + lax.axis_index("mirror")
    count_here = jnp.sum(jnp.where(cluster_ids == owner, counts, 0)).astype(f32)
    cosine = jnp.dot(members, members.T, preferred_element_type=f32)
    index = jnp.arange(width, dtype=jnp.int32)
    weights = jnp.where(
        index[:, None] == index[None, :],
        0.0,
        jnp.exp(sharpness * cosine) * valid.astype(f32)[None, :],
    )
    total = jnp.sum(weights, axis=1)
    scores = jnp.log(1.0 + total / count_here).reshape(shard_count, mirror_count, capacity)
    dup_score = exchange(scores).reshape(width)[flat_slot]
    onehot_home = (assignment[:, None] == cluster_ids[None, :]).astype(bf16)
    partial_value = jnp.einsum("rk,rd->kd", onehot_home, unit_rows, preferred_element_type=f32)
    own_sum = lax.psum_scatter(partial_value, ("shard", "mirror"), scatter_dimension=0, tiled=True)
    own_centroid = own_sum / jnp.sqrt(jnp.mean(own_sum * own_sum, axis=1, keepdims=True) + 1e-06)
    centroids = lax.all_gather(own_centroid, ("shard", "mirror"), axis=0, tiled=True)
    return (dup_score, centroids)


def local(embeddings, assignment, counts, slot):
    devices_here = lax.axis_size("shard") * lax.axis_size("mirror")
    capacity = max(2, (2 * embeddings.shape[0] + devices_here - 1) // devices_here)
    powers = devices_here & (devices_here - 1) == 0 and devices_here % 4 == 0
    whole_tiles = capacity % 16 == 0 and (2 * capacity) % 128 == 0
    form = fused if powers and whole_tiles and counts.shape[0] == devices_here else general
    return form(embeddings, assignment, counts, slot, capacity)


def solution(mesh):
    placed = (
        P(("groups", "shard", "mirror"), None),
        P(("groups", "shard", "mirror")),
        P("groups"),
        P(("groups", "shard", "mirror")),
    )
    return jax.shard_map(
        local,
        mesh=mesh,
        in_specs=placed,
        out_specs=(P(("groups", "shard", "mirror")), P("groups", None)),
        check_vma=False,
    )
```

```python
import functools

import jax
import jax.numpy as jnp
from jax import lax
from jax.experimental import pallas as pl
from jax.experimental.pallas import tpu as pltpu
from jax.sharding import PartitionSpec as P

sharpness = 50.0
f32, bf16 = jnp.float32, jnp.bfloat16


def flipped(index, mask):
    result, place = index, 1
    while place <= mask:
        if mask & place:
            bit = lax.rem(lax.div(index, place), 2)
            result = result + place * (1 - 2 * bit)
        place *= 2
    return result


def kernel(
    shards,
    mirrors,
    sends,
    emb_hbm,
    assign_hbm,
    slot_hbm,
    counts_hbm,
    score_ref,
    cent_ref,
    emb,
    assign,
    slot,
    counts,
    place,
    outgoing,
    members,
    across,
    down,
    reply_out,
    reply_in,
    load_sem,
    row_send,
    row_recv,
    reply_send,
    reply_recv,
):
    n = shards * mirrors
    rows, features = emb.shape
    width = members.shape[0]
    cap = width // n
    pair = 2 * cap
    my_shard, my_mirror = lax.axis_index("shard"), lax.axis_index("mirror")
    me = my_shard * mirrors + my_mirror

    def peer(q):
        return {
            "shard": flipped(my_shard, q // mirrors),
            "mirror": flipped(my_mirror, q % mirrors),
        }

    def remote(src, dst, send, recv, q):
        return pltpu.make_async_remote_copy(
            src_ref=src,
            dst_ref=dst,
            send_sem=send.at[q],
            recv_sem=recv.at[q],
            device_id=peer(q),
            device_id_type=pl.DeviceIdType.MESH,
        )

    loads = [
        pltpu.make_async_copy(src, dst, load_sem.at[k])
        for k, (src, dst) in enumerate(
            [(assign_hbm, assign), (slot_hbm, slot), (emb_hbm, emb), (counts_hbm, counts)]
        )
    ]
    for load in loads:
        load.start()
    barrier = pltpu.get_barrier_semaphore()
    for q in range(1, n):
        pl.semaphore_signal(
            barrier, inc=1, device_id=peer(q), device_id_type=pl.DeviceIdType.MESH
        )
    for load in loads:
        load.wait()

    flat_slot = (assign[...] ^ me) * cap + slot[...]
    row_copies = {
        q: remote(
            outgoing.at[pl.ds(q * cap, cap)],
            members.at[pl.ds(q * cap, cap)],
            row_send,
            row_recv,
            q,
        )
        for q in range(1, n)
    }
    span = mirrors * cap
    for turn, dz in enumerate(sends):
        first = dz * mirrors
        slots = lax.broadcasted_iota(jnp.int32, (span, rows), 0) + first * cap
        hot = jnp.where(slots == flat_slot, 1.0, 0.0).astype(bf16)
        place[pl.ds(first * cap, span), :] = hot
        block = jnp.dot(hot, emb[...], preferred_element_type=f32).astype(bf16)
        if first == 0:
            members[pl.ds(0, cap), :] = block[:cap]
            outgoing[pl.ds(cap, span - cap), :] = block[cap:]
        else:
            outgoing[pl.ds(first * cap, span), :] = block
        if turn == 0:
            pl.semaphore_wait(barrier, n - 1)
        for q in range(max(first, 1), first + mirrors):
            row_copies[q].start()

    count = jnp.sum(
        jnp.where(lax.broadcasted_iota(jnp.int32, counts.shape, 1) == me, counts[...], 0),
        axis=1,
        keepdims=True,
    ).astype(f32)

    def fold(x):
        return jnp.sum(x.reshape(x.shape[0] // 8, 8, x.shape[1]), axis=0)

    own = lax.broadcasted_iota(jnp.int32, (pair, pair), 0) == lax.broadcasted_iota(
        jnp.int32, (pair, pair), 1
    )
    sums = jnp.zeros((8, features), f32)
    for p in range(n // 2):
        for q in (2 * p, 2 * p + 1):
            if q > 0:
                row_copies[q].wait_recv()
        wide = members[pl.ds(p * pair, pair), :].astype(f32)
        square = jnp.sum(wide * wide, axis=1, keepdims=True) + 1e-06
        fresh = (wide * (1.0 / jnp.sqrt(square))).astype(bf16)
        members[pl.ds(p * pair, pair), :] = fresh
        sums = sums + fold(fresh.astype(f32))
        cosine = lax.dot_general(
            members[pl.ds(0, (p + 1) * pair), :],
            fresh,
            (((1,), (1,)), ((), ())),
            preferred_element_type=f32,
        )
        grown = jnp.exp(sharpness * cosine) - 1.0
        within = jnp.where(own, 0.0, grown[p * pair :])
        if p > 0:
            across[pl.ds(0, p * pair), :] += grown[: p * pair]
            within_and_old = fold(within) + fold(grown[: p * pair])
        else:
            within_and_old = fold(within)
        across[pl.ds(p * pair, pair), :] = jnp.zeros((pair, pair), f32)
        down[:, pl.ds(p * pair, pair)] = within_and_old

    sum_row = jnp.sum(sums, axis=0, keepdims=True)
    centroid = sum_row / jnp.sqrt(jnp.mean(sum_row * sum_row, axis=1, keepdims=True) + 1e-06)

    lanes = across[...]
    high = lanes.astype(bf16)
    low = (lanes - high.astype(f32)).astype(bf16)
    ones = jnp.ones((16, 2 * pair), bf16)
    turned = lax.dot_general(
        ones,
        jnp.concatenate([high, low], axis=1),
        (((1,), (1,)), ((), ())),
        preferred_element_type=f32,
    )
    sum_here = jnp.sum(down[...], axis=0, keepdims=True) + turned[0:1] + (count - 1.0)
    scores = jnp.log(1.0 + sum_here / count)
    for p in range(n // 2):
        reply_out[p] = jnp.concatenate([centroid, scores[:, p * pair : (p + 1) * pair]], axis=1)
    reply_copies = {
        q: remote(reply_out.at[q // 2], reply_in.at[q], reply_send, reply_recv, q)
        for q in range(1, n)
    }
    for q in range(n - 1, 0, -1):
        reply_copies[q].start()
    reply_in[0] = reply_out[0]
    for q in range(1, n):
        row_copies[q].wait_send()
    for q in range(1, n):
        reply_copies[q].wait_recv()
    first_half = lax.broadcasted_iota(jnp.int32, (1, pair), 1) < cap
    returned = jnp.concatenate(
        [
            jnp.where(first_half, reply_in[2 * p, :, features:], reply_in[2 * p + 1, :, features:])
            for p in range(n // 2)
        ],
        axis=1,
    )
    high = returned.astype(bf16)
    rest = returned - high.astype(f32)
    middle = rest.astype(bf16)
    little = (rest - middle.astype(f32)).astype(bf16)
    terms = jnp.concatenate([high, middle, little, jnp.zeros((13, width), bf16)], axis=0)
    picked = jnp.dot(terms, place[...], preferred_element_type=f32)
    score_ref[...] = picked[0:1] + (picked[1:2] + picked[2:3])
    for q in range(n):
        there = peer(q)
        cluster = there["shard"] * mirrors + there["mirror"]
        cent_ref[pl.ds(cluster, 1), :] = reply_in[q, :, :features]
    for q in range(1, n):
        reply_copies[q].wait_send()


def fused(embeddings, assignment, counts, slot, capacity):
    shards, mirrors = lax.axis_size("shard"), lax.axis_size("mirror")
    n = shards * mirrors
    rows, features = embeddings.shape
    width = n * capacity
    pair = 2 * capacity
    vmem = pl.BlockSpec(memory_space=pltpu.VMEM)
    anywhere = pl.BlockSpec(memory_space=pl.ANY)
    half = max(1, shards // 2)
    sends = sorted(range(shards), key=lambda dz: (dz % half, -dz))
    scores, centroids = pl.pallas_call(
        functools.partial(kernel, shards, mirrors, sends),
        out_shape=(
            jax.ShapeDtypeStruct((1, rows), f32),
            jax.ShapeDtypeStruct((n, features), f32),
        ),
        in_specs=[anywhere] * 4,
        out_specs=(vmem, vmem),
        scratch_shapes=[
            pltpu.VMEM((rows, features), bf16),
            pltpu.VMEM((1, rows), jnp.int32),
            pltpu.VMEM((1, rows), jnp.int32),
            pltpu.VMEM((1, n), jnp.int32),
            pltpu.VMEM((width, rows), bf16),
            pltpu.VMEM((width, features), bf16),
            pltpu.VMEM((width, features), bf16),
            pltpu.VMEM((width, pair), f32),
            pltpu.VMEM((8, width), f32),
            pltpu.VMEM((n // 2, 1, features + pair), f32),
            pltpu.VMEM((n, 1, features + pair), f32),
            pltpu.SemaphoreType.DMA((4,)),
        ]
        + [pltpu.SemaphoreType.DMA((n,))] * 4,
        compiler_params=pltpu.CompilerParams(
            collective_id=0, has_side_effects=True, vmem_limit_bytes=40 * 2**20
        ),
    )(embeddings, assignment[None, :], slot[None, :], counts[None, :])
    return scores.reshape(rows), centroids


def general(embeddings, assignment, counts, slot, capacity):
    shard_count = lax.axis_size("shard")
    mirror_count = lax.axis_size("mirror")
    rows_here, features = embeddings.shape
    clusters = counts.shape[0]
    width = shard_count * mirror_count * capacity

    def exchange(x):
        x = lax.all_to_all(x, "shard", split_axis=0, concat_axis=0, tiled=True)
        return lax.all_to_all(x, "mirror", split_axis=1, concat_axis=1, tiled=True)

    wide = embeddings.astype(f32)
    unit_rows = (wide / jnp.sqrt(jnp.sum(wide * wide, axis=1, keepdims=True) + 1e-06)).astype(bf16)
    cluster_ids = jnp.arange(clusters, dtype=jnp.int32)
    flat_slot = assignment * capacity + slot
    outgoing = jnp.zeros((width, features), bf16).at[flat_slot].set(unit_rows)
    present = jnp.zeros((width,), bf16).at[flat_slot].set(jnp.ones((rows_here,), bf16))
    members = exchange(outgoing.reshape(shard_count, mirror_count, capacity, features)).reshape(
        width, features
    )
    valid = exchange(present.reshape(shard_count, mirror_count, capacity)).reshape(width)
    owner = lax.axis_index("shard") * mirror_count + lax.axis_index("mirror")
    count_here = jnp.sum(jnp.where(cluster_ids == owner, counts, 0)).astype(f32)
    cosine = jnp.dot(members, members.T, preferred_element_type=f32)
    index = jnp.arange(width, dtype=jnp.int32)
    weights = jnp.where(
        index[:, None] == index[None, :],
        0.0,
        jnp.exp(sharpness * cosine) * valid.astype(f32)[None, :],
    )
    total = jnp.sum(weights, axis=1)
    scores = jnp.log(1.0 + total / count_here).reshape(shard_count, mirror_count, capacity)
    dup_score = exchange(scores).reshape(width)[flat_slot]
    onehot_home = (assignment[:, None] == cluster_ids[None, :]).astype(bf16)
    partial_value = jnp.einsum("rk,rd->kd", onehot_home, unit_rows, preferred_element_type=f32)
    own_sum = lax.psum_scatter(partial_value, ("shard", "mirror"), scatter_dimension=0, tiled=True)
    own_centroid = own_sum / jnp.sqrt(jnp.mean(own_sum * own_sum, axis=1, keepdims=True) + 1e-06)
    centroids = lax.all_gather(own_centroid, ("shard", "mirror"), axis=0, tiled=True)
    return (dup_score, centroids)


def local(embeddings, assignment, counts, slot):
    devices_here = lax.axis_size("shard") * lax.axis_size("mirror")
    capacity = max(2, (2 * embeddings.shape[0] + devices_here - 1) // devices_here)
    powers = devices_here & (devices_here - 1) == 0 and devices_here % 4 == 0
    whole_tiles = capacity % 16 == 0 and (2 * capacity) % 128 == 0
    form = fused if powers and whole_tiles and counts.shape[0] == devices_here else general
    return form(embeddings, assignment, counts, slot, capacity)


def solution(mesh):
    placed = (
        P(("groups", "shard", "mirror"), None),
        P(("groups", "shard", "mirror")),
        P("groups"),
        P(("groups", "shard", "mirror")),
    )
    return jax.shard_map(
        local,
        mesh=mesh,
        in_specs=placed,
        out_specs=(P(("groups", "shard", "mirror")), P("groups", None)),
        check_vma=False,
    )
```

```python
import functools

import jax
import jax.numpy as jnp
from jax import lax
from jax.experimental import pallas as pl
from jax.experimental.pallas import tpu as pltpu
from jax.sharding import PartitionSpec as P

sharpness = 50.0
f32, bf16 = jnp.float32, jnp.bfloat16


def flipped(index, mask):
    result, place = index, 1
    while place <= mask:
        if mask & place:
            bit = lax.rem(lax.div(index, place), 2)
            result = result + place * (1 - 2 * bit)
        place *= 2
    return result


def kernel(
    shards,
    mirrors,
    sends,
    emb_hbm,
    assign_hbm,
    slot_hbm,
    counts_hbm,
    score_ref,
    cent_ref,
    emb,
    assign,
    slot,
    counts,
    place,
    outgoing,
    members,
    across,
    down,
    reply_out,
    reply_in,
    load_sem,
    row_send,
    row_recv,
    reply_send,
    reply_recv,
):
    n = shards * mirrors
    rows, features = emb.shape
    width = members.shape[0]
    cap = width // n
    pair = 2 * cap
    my_shard, my_mirror = lax.axis_index("shard"), lax.axis_index("mirror")
    me = my_shard * mirrors + my_mirror

    def peer(q):
        return {
            "shard": flipped(my_shard, q // mirrors),
            "mirror": flipped(my_mirror, q % mirrors),
        }

    def remote(src, dst, send, recv, q):
        return pltpu.make_async_remote_copy(
            src_ref=src,
            dst_ref=dst,
            send_sem=send.at[q],
            recv_sem=recv.at[q],
            device_id=peer(q),
            device_id_type=pl.DeviceIdType.MESH,
        )

    loads = [
        pltpu.make_async_copy(src, dst, load_sem.at[k])
        for k, (src, dst) in enumerate(
            [(emb_hbm, emb), (assign_hbm, assign), (slot_hbm, slot), (counts_hbm, counts)]
        )
    ]
    for load in loads:
        load.start()
    barrier = pltpu.get_barrier_semaphore()
    for q in range(1, n):
        pl.semaphore_signal(
            barrier, inc=1, device_id=peer(q), device_id_type=pl.DeviceIdType.MESH
        )
    for load in loads[1:]:
        load.wait()

    flat_slot = (assign[...] ^ me) * cap + slot[...]
    row_copies = {
        q: remote(
            outgoing.at[pl.ds(q * cap, cap)],
            members.at[pl.ds(q * cap, cap)],
            row_send,
            row_recv,
            q,
        )
        for q in range(1, n)
    }
    span = mirrors * cap
    for turn, dz in enumerate(sends):
        first = dz * mirrors
        slots = lax.broadcasted_iota(jnp.int32, (span, rows), 0) + first * cap
        hot = jnp.where(slots == flat_slot, 1.0, 0.0).astype(bf16)
        place[pl.ds(first * cap, span), :] = hot
        if turn == 0:
            loads[0].wait()
        block = jnp.dot(hot, emb[...], preferred_element_type=f32).astype(bf16)
        if first == 0:
            members[pl.ds(0, cap), :] = block[:cap]
            outgoing[pl.ds(cap, span - cap), :] = block[cap:]
        else:
            outgoing[pl.ds(first * cap, span), :] = block
        if turn == 0:
            pl.semaphore_wait(barrier, n - 1)
        for q in range(max(first, 1), first + mirrors):
            row_copies[q].start()

    count = jnp.sum(
        jnp.where(lax.broadcasted_iota(jnp.int32, counts.shape, 1) == me, counts[...], 0),
        axis=1,
        keepdims=True,
    ).astype(f32)

    def fold(x):
        return jnp.sum(x.reshape(x.shape[0] // 8, 8, x.shape[1]), axis=0)

    own = lax.broadcasted_iota(jnp.int32, (pair, pair), 0) == lax.broadcasted_iota(
        jnp.int32, (pair, pair), 1
    )
    sums = jnp.zeros((8, features), f32)
    for p in range(n // 2):
        for q in (2 * p, 2 * p + 1):
            if q > 0:
                row_copies[q].wait_recv()
        wide = members[pl.ds(p * pair, pair), :].astype(f32)
        square = jnp.sum(wide * wide, axis=1, keepdims=True) + 1e-06
        fresh = (wide * (1.0 / jnp.sqrt(square))).astype(bf16)
        members[pl.ds(p * pair, pair), :] = fresh
        sums = sums + fold(fresh.astype(f32))
        cosine = lax.dot_general(
            members[pl.ds(0, (p + 1) * pair), :],
            fresh,
            (((1,), (1,)), ((), ())),
            preferred_element_type=f32,
        )
        grown = jnp.exp(sharpness * cosine) - 1.0
        within = jnp.where(own, 0.0, grown[p * pair :])
        if p > 0:
            across[pl.ds(0, p * pair), :] += grown[: p * pair]
            within_and_old = fold(within) + fold(grown[: p * pair])
        else:
            within_and_old = fold(within)
        across[pl.ds(p * pair, pair), :] = jnp.zeros((pair, pair), f32)
        down[:, pl.ds(p * pair, pair)] = within_and_old

    sum_row = jnp.sum(sums, axis=0, keepdims=True)
    centroid = sum_row / jnp.sqrt(jnp.mean(sum_row * sum_row, axis=1, keepdims=True) + 1e-06)

    lanes = across[...]
    high = lanes.astype(bf16)
    low = (lanes - high.astype(f32)).astype(bf16)
    ones = jnp.ones((16, 2 * pair), bf16)
    turned = lax.dot_general(
        ones,
        jnp.concatenate([high, low], axis=1),
        (((1,), (1,)), ((), ())),
        preferred_element_type=f32,
    )
    sum_here = jnp.sum(down[...], axis=0, keepdims=True) + turned[0:1] + (count - 1.0)
    scores = jnp.log(1.0 + sum_here / count)
    for p in range(n // 2):
        reply_out[p] = jnp.concatenate([centroid, scores[:, p * pair : (p + 1) * pair]], axis=1)
    reply_copies = {
        q: remote(reply_out.at[q // 2], reply_in.at[q], reply_send, reply_recv, q)
        for q in range(1, n)
    }
    for q in range(n - 1, 0, -1):
        reply_copies[q].start()
    reply_in[0] = reply_out[0]
    for q in range(1, n):
        row_copies[q].wait_send()
    for q in range(1, n):
        reply_copies[q].wait_recv()
    first_half = lax.broadcasted_iota(jnp.int32, (1, pair), 1) < cap
    returned = jnp.concatenate(
        [
            jnp.where(first_half, reply_in[2 * p, :, features:], reply_in[2 * p + 1, :, features:])
            for p in range(n // 2)
        ],
        axis=1,
    )
    high = returned.astype(bf16)
    rest = returned - high.astype(f32)
    middle = rest.astype(bf16)
    little = (rest - middle.astype(f32)).astype(bf16)
    terms = jnp.concatenate([high, middle, little, jnp.zeros((13, width), bf16)], axis=0)
    picked = jnp.dot(terms, place[...], preferred_element_type=f32)
    score_ref[...] = picked[0:1] + (picked[1:2] + picked[2:3])
    for q in range(n):
        there = peer(q)
        cluster = there["shard"] * mirrors + there["mirror"]
        cent_ref[pl.ds(cluster, 1), :] = reply_in[q, :, :features]
    for q in range(1, n):
        reply_copies[q].wait_send()


def fused(embeddings, assignment, counts, slot, capacity):
    shards, mirrors = lax.axis_size("shard"), lax.axis_size("mirror")
    n = shards * mirrors
    rows, features = embeddings.shape
    width = n * capacity
    pair = 2 * capacity
    vmem = pl.BlockSpec(memory_space=pltpu.VMEM)
    anywhere = pl.BlockSpec(memory_space=pl.ANY)
    half = max(1, shards // 2)
    sends = sorted(range(shards), key=lambda dz: (dz % half, -dz))
    scores, centroids = pl.pallas_call(
        functools.partial(kernel, shards, mirrors, sends),
        out_shape=(
            jax.ShapeDtypeStruct((1, rows), f32),
            jax.ShapeDtypeStruct((n, features), f32),
        ),
        in_specs=[anywhere] * 4,
        out_specs=(vmem, vmem),
        scratch_shapes=[
            pltpu.VMEM((rows, features), bf16),
            pltpu.VMEM((1, rows), jnp.int32),
            pltpu.VMEM((1, rows), jnp.int32),
            pltpu.VMEM((1, n), jnp.int32),
            pltpu.VMEM((width, rows), bf16),
            pltpu.VMEM((width, features), bf16),
            pltpu.VMEM((width, features), bf16),
            pltpu.VMEM((width, pair), f32),
            pltpu.VMEM((8, width), f32),
            pltpu.VMEM((n // 2, 1, features + pair), f32),
            pltpu.VMEM((n, 1, features + pair), f32),
            pltpu.SemaphoreType.DMA((4,)),
        ]
        + [pltpu.SemaphoreType.DMA((n,))] * 4,
        compiler_params=pltpu.CompilerParams(
            collective_id=0, has_side_effects=True, vmem_limit_bytes=40 * 2**20
        ),
    )(embeddings, assignment[None, :], slot[None, :], counts[None, :])
    return scores.reshape(rows), centroids


def general(embeddings, assignment, counts, slot, capacity):
    shard_count = lax.axis_size("shard")
    mirror_count = lax.axis_size("mirror")
    rows_here, features = embeddings.shape
    clusters = counts.shape[0]
    width = shard_count * mirror_count * capacity

    def exchange(x):
        x = lax.all_to_all(x, "shard", split_axis=0, concat_axis=0, tiled=True)
        return lax.all_to_all(x, "mirror", split_axis=1, concat_axis=1, tiled=True)

    wide = embeddings.astype(f32)
    unit_rows = (wide / jnp.sqrt(jnp.sum(wide * wide, axis=1, keepdims=True) + 1e-06)).astype(bf16)
    cluster_ids = jnp.arange(clusters, dtype=jnp.int32)
    flat_slot = assignment * capacity + slot
    outgoing = jnp.zeros((width, features), bf16).at[flat_slot].set(unit_rows)
    present = jnp.zeros((width,), bf16).at[flat_slot].set(jnp.ones((rows_here,), bf16))
    members = exchange(outgoing.reshape(shard_count, mirror_count, capacity, features)).reshape(
        width, features
    )
    valid = exchange(present.reshape(shard_count, mirror_count, capacity)).reshape(width)
    owner = lax.axis_index("shard") * mirror_count + lax.axis_index("mirror")
    count_here = jnp.sum(jnp.where(cluster_ids == owner, counts, 0)).astype(f32)
    cosine = jnp.dot(members, members.T, preferred_element_type=f32)
    index = jnp.arange(width, dtype=jnp.int32)
    weights = jnp.where(
        index[:, None] == index[None, :],
        0.0,
        jnp.exp(sharpness * cosine) * valid.astype(f32)[None, :],
    )
    total = jnp.sum(weights, axis=1)
    scores = jnp.log(1.0 + total / count_here).reshape(shard_count, mirror_count, capacity)
    dup_score = exchange(scores).reshape(width)[flat_slot]
    onehot_home = (assignment[:, None] == cluster_ids[None, :]).astype(bf16)
    partial_value = jnp.einsum("rk,rd->kd", onehot_home, unit_rows, preferred_element_type=f32)
    own_sum = lax.psum_scatter(partial_value, ("shard", "mirror"), scatter_dimension=0, tiled=True)
    own_centroid = own_sum / jnp.sqrt(jnp.mean(own_sum * own_sum, axis=1, keepdims=True) + 1e-06)
    centroids = lax.all_gather(own_centroid, ("shard", "mirror"), axis=0, tiled=True)
    return (dup_score, centroids)


def local(embeddings, assignment, counts, slot):
    devices_here = lax.axis_size("shard") * lax.axis_size("mirror")
    capacity = max(2, (2 * embeddings.shape[0] + devices_here - 1) // devices_here)
    powers = devices_here & (devices_here - 1) == 0 and devices_here % 4 == 0
    whole_tiles = capacity % 16 == 0 and (2 * capacity) % 128 == 0
    form = fused if powers and whole_tiles and counts.shape[0] == devices_here else general
    return form(embeddings, assignment, counts, slot, capacity)


def solution(mesh):
    placed = (
        P(("groups", "shard", "mirror"), None),
        P(("groups", "shard", "mirror")),
        P("groups"),
        P(("groups", "shard", "mirror")),
    )
    return jax.shard_map(
        local,
        mesh=mesh,
        in_specs=placed,
        out_specs=(P(("groups", "shard", "mirror")), P("groups", None)),
        check_vma=False,
    )
```

```python
import functools

import jax
import jax.numpy as jnp
from jax import lax
from jax.experimental import pallas as pl
from jax.experimental.pallas import tpu as pltpu
from jax.sharding import PartitionSpec as P

sharpness = 50.0
f32, bf16 = jnp.float32, jnp.bfloat16


def flipped(index, mask):
    result, place = index, 1
    while place <= mask:
        if mask & place:
            bit = lax.rem(lax.div(index, place), 2)
            result = result + place * (1 - 2 * bit)
        place *= 2
    return result


def kernel(
    shards,
    mirrors,
    sends,
    emb,
    assign,
    slot,
    counts,
    score_ref,
    cent_ref,
    place,
    outgoing,
    members,
    across,
    down,
    reply_out,
    reply_in,
    row_send,
    row_recv,
    reply_send,
    reply_recv,
):
    n = shards * mirrors
    rows, features = emb.shape
    width = members.shape[0]
    cap = width // n
    pair = 2 * cap
    my_shard, my_mirror = lax.axis_index("shard"), lax.axis_index("mirror")
    me = my_shard * mirrors + my_mirror

    def peer(q):
        return {
            "shard": flipped(my_shard, q // mirrors),
            "mirror": flipped(my_mirror, q % mirrors),
        }

    def remote(src, dst, send, recv, q):
        return pltpu.make_async_remote_copy(
            src_ref=src,
            dst_ref=dst,
            send_sem=send.at[q],
            recv_sem=recv.at[q],
            device_id=peer(q),
            device_id_type=pl.DeviceIdType.MESH,
        )

    barrier = pltpu.get_barrier_semaphore()
    for q in range(1, n):
        pl.semaphore_signal(
            barrier, inc=1, device_id=peer(q), device_id_type=pl.DeviceIdType.MESH
        )

    flat_slot = (assign[...] ^ me) * cap + slot[...]
    row_copies = {
        q: remote(
            outgoing.at[pl.ds(q * cap, cap)],
            members.at[pl.ds(q * cap, cap)],
            row_send,
            row_recv,
            q,
        )
        for q in range(1, n)
    }
    span = mirrors * cap
    for turn, dz in enumerate(sends):
        first = dz * mirrors
        slots = lax.broadcasted_iota(jnp.int32, (span, rows), 0) + first * cap
        hot = jnp.where(slots == flat_slot, 1.0, 0.0).astype(bf16)
        place[pl.ds(first * cap, span), :] = hot
        block = jnp.dot(hot, emb[...], preferred_element_type=f32).astype(bf16)
        if first == 0:
            members[pl.ds(0, cap), :] = block[:cap]
            outgoing[pl.ds(cap, span - cap), :] = block[cap:]
        else:
            outgoing[pl.ds(first * cap, span), :] = block
        if turn == 0:
            pl.semaphore_wait(barrier, n - 1)
        for q in range(max(first, 1), first + mirrors):
            row_copies[q].start()

    count = jnp.sum(
        jnp.where(lax.broadcasted_iota(jnp.int32, counts.shape, 1) == me, counts[...], 0),
        axis=1,
        keepdims=True,
    ).astype(f32)

    def fold(x):
        return jnp.sum(x.reshape(x.shape[0] // 8, 8, x.shape[1]), axis=0)

    own = lax.broadcasted_iota(jnp.int32, (pair, pair), 0) == lax.broadcasted_iota(
        jnp.int32, (pair, pair), 1
    )
    sums = jnp.zeros((8, features), f32)
    for p in range(n // 2):
        for q in (2 * p, 2 * p + 1):
            if q > 0:
                row_copies[q].wait_recv()
        wide = members[pl.ds(p * pair, pair), :].astype(f32)
        square = jnp.sum(wide * wide, axis=1, keepdims=True) + 1e-06
        fresh = (wide * (1.0 / jnp.sqrt(square))).astype(bf16)
        members[pl.ds(p * pair, pair), :] = fresh
        sums = sums + fold(fresh.astype(f32))
        cosine = lax.dot_general(
            members[pl.ds(0, (p + 1) * pair), :],
            fresh,
            (((1,), (1,)), ((), ())),
            preferred_element_type=f32,
        )
        grown = jnp.exp(sharpness * cosine) - 1.0
        within = jnp.where(own, 0.0, grown[p * pair :])
        if p > 0:
            across[pl.ds(0, p * pair), :] += grown[: p * pair]
            within_and_old = fold(within) + fold(grown[: p * pair])
        else:
            within_and_old = fold(within)
        across[pl.ds(p * pair, pair), :] = jnp.zeros((pair, pair), f32)
        down[:, pl.ds(p * pair, pair)] = within_and_old

    sum_row = jnp.sum(sums, axis=0, keepdims=True)
    centroid = sum_row / jnp.sqrt(jnp.mean(sum_row * sum_row, axis=1, keepdims=True) + 1e-06)

    lanes = across[...]
    high = lanes.astype(bf16)
    low = (lanes - high.astype(f32)).astype(bf16)
    ones = jnp.ones((16, 2 * pair), bf16)
    turned = lax.dot_general(
        ones,
        jnp.concatenate([high, low], axis=1),
        (((1,), (1,)), ((), ())),
        preferred_element_type=f32,
    )
    sum_here = jnp.sum(down[...], axis=0, keepdims=True) + turned[0:1] + (count - 1.0)
    scores = jnp.log(1.0 + sum_here / count)
    for p in range(n // 2):
        reply_out[p] = jnp.concatenate([centroid, scores[:, p * pair : (p + 1) * pair]], axis=1)
    reply_copies = {
        q: remote(reply_out.at[q // 2], reply_in.at[q], reply_send, reply_recv, q)
        for q in range(1, n)
    }
    for q in range(n - 1, 0, -1):
        reply_copies[q].start()
    reply_in[0] = reply_out[0]
    for q in range(1, n):
        row_copies[q].wait_send()
    for q in range(1, n):
        reply_copies[q].wait_recv()
    first_half = lax.broadcasted_iota(jnp.int32, (1, pair), 1) < cap
    returned = jnp.concatenate(
        [
            jnp.where(first_half, reply_in[2 * p, :, features:], reply_in[2 * p + 1, :, features:])
            for p in range(n // 2)
        ],
        axis=1,
    )
    high = returned.astype(bf16)
    rest = returned - high.astype(f32)
    middle = rest.astype(bf16)
    little = (rest - middle.astype(f32)).astype(bf16)
    terms = jnp.concatenate([high, middle, little, jnp.zeros((13, width), bf16)], axis=0)
    picked = jnp.dot(terms, place[...], preferred_element_type=f32)
    score_ref[...] = picked[0:1] + (picked[1:2] + picked[2:3])
    for q in range(n):
        there = peer(q)
        cluster = there["shard"] * mirrors + there["mirror"]
        cent_ref[pl.ds(cluster, 1), :] = reply_in[q, :, :features]
    for q in range(1, n):
        reply_copies[q].wait_send()


def fused(embeddings, assignment, counts, slot, capacity):
    shards, mirrors = lax.axis_size("shard"), lax.axis_size("mirror")
    n = shards * mirrors
    rows, features = embeddings.shape
    width = n * capacity
    pair = 2 * capacity
    vmem = pl.BlockSpec(memory_space=pltpu.VMEM)
    half = max(1, shards // 2)
    sends = sorted(range(shards), key=lambda dz: (dz % half, -dz))
    scores, centroids = pl.pallas_call(
        functools.partial(kernel, shards, mirrors, sends),
        out_shape=(
            jax.ShapeDtypeStruct((1, rows), f32),
            jax.ShapeDtypeStruct((n, features), f32),
        ),
        in_specs=[vmem] * 4,
        out_specs=(vmem, vmem),
        scratch_shapes=[
            pltpu.VMEM((width, rows), bf16),
            pltpu.VMEM((width, features), bf16),
            pltpu.VMEM((width, features), bf16),
            pltpu.VMEM((width, pair), f32),
            pltpu.VMEM((8, width), f32),
            pltpu.VMEM((n // 2, 1, features + pair), f32),
            pltpu.VMEM((n, 1, features + pair), f32),
        ]
        + [pltpu.SemaphoreType.DMA((n,))] * 4,
        compiler_params=pltpu.CompilerParams(
            collective_id=0, has_side_effects=True, vmem_limit_bytes=40 * 2**20
        ),
    )(embeddings, assignment[None, :], slot[None, :], counts[None, :])
    return scores.reshape(rows), centroids


def general(embeddings, assignment, counts, slot, capacity):
    shard_count = lax.axis_size("shard")
    mirror_count = lax.axis_size("mirror")
    rows_here, features = embeddings.shape
    clusters = counts.shape[0]
    width = shard_count * mirror_count * capacity

    def exchange(x):
        x = lax.all_to_all(x, "shard", split_axis=0, concat_axis=0, tiled=True)
        return lax.all_to_all(x, "mirror", split_axis=1, concat_axis=1, tiled=True)

    wide = embeddings.astype(f32)
    unit_rows = (wide / jnp.sqrt(jnp.sum(wide * wide, axis=1, keepdims=True) + 1e-06)).astype(bf16)
    cluster_ids = jnp.arange(clusters, dtype=jnp.int32)
    flat_slot = assignment * capacity + slot
    outgoing = jnp.zeros((width, features), bf16).at[flat_slot].set(unit_rows)
    present = jnp.zeros((width,), bf16).at[flat_slot].set(jnp.ones((rows_here,), bf16))
    members = exchange(outgoing.reshape(shard_count, mirror_count, capacity, features)).reshape(
        width, features
    )
    valid = exchange(present.reshape(shard_count, mirror_count, capacity)).reshape(width)
    owner = lax.axis_index("shard") * mirror_count + lax.axis_index("mirror")
    count_here = jnp.sum(jnp.where(cluster_ids == owner, counts, 0)).astype(f32)
    cosine = jnp.dot(members, members.T, preferred_element_type=f32)
    index = jnp.arange(width, dtype=jnp.int32)
    weights = jnp.where(
        index[:, None] == index[None, :],
        0.0,
        jnp.exp(sharpness * cosine) * valid.astype(f32)[None, :],
    )
    total = jnp.sum(weights, axis=1)
    scores = jnp.log(1.0 + total / count_here).reshape(shard_count, mirror_count, capacity)
    dup_score = exchange(scores).reshape(width)[flat_slot]
    onehot_home = (assignment[:, None] == cluster_ids[None, :]).astype(bf16)
    partial_value = jnp.einsum("rk,rd->kd", onehot_home, unit_rows, preferred_element_type=f32)
    own_sum = lax.psum_scatter(partial_value, ("shard", "mirror"), scatter_dimension=0, tiled=True)
    own_centroid = own_sum / jnp.sqrt(jnp.mean(own_sum * own_sum, axis=1, keepdims=True) + 1e-06)
    centroids = lax.all_gather(own_centroid, ("shard", "mirror"), axis=0, tiled=True)
    return (dup_score, centroids)


def local(embeddings, assignment, counts, slot):
    devices_here = lax.axis_size("shard") * lax.axis_size("mirror")
    capacity = max(2, (2 * embeddings.shape[0] + devices_here - 1) // devices_here)
    powers = devices_here & (devices_here - 1) == 0 and devices_here % 4 == 0
    whole_tiles = capacity % 16 == 0 and (2 * capacity) % 128 == 0
    form = fused if powers and whole_tiles and counts.shape[0] == devices_here else general
    return form(embeddings, assignment, counts, slot, capacity)


def solution(mesh):
    placed = (
        P(("groups", "shard", "mirror"), None),
        P(("groups", "shard", "mirror")),
        P("groups"),
        P(("groups", "shard", "mirror")),
    )
    return jax.shard_map(
        local,
        mesh=mesh,
        in_specs=placed,
        out_specs=(P(("groups", "shard", "mirror")), P("groups", None)),
        check_vma=False,
    )
```
